32 devices in a mesh: cen: 16 (over z, y, core), out: 2 (over x).
Axes of the slice: x: 2, y: 2, z: 4, core: 2. Of those that a mesh axis runs over, the one named last changes fastest.
Arguments:
- features: float32 [32768, 1024], P('cen', 'out'), may hold values from -6 to 6
- centres: float32 [32768, 1024], P('cen', 'out'), may hold values from -6 to 6
- coefs: float32 [32768, 1000], P('cen', 'out'), may hold values from -0.0625 to 0.0625
- batch_index: int32 [2, 256], P(None, 'cen'), may hold values from 0 to 2047
- targets: float32 [2, 256, 1000], P(None, 'cen', 'out'), may hold values from -6 to 6
Outputs:
- residuals: float32 [2, 256, 1000], P(None, 'cen', 'out')
- new_coefs: float32 [32768, 1000], P('cen', 'out')
The draws below stay inside these ranges and needn't reach their ends.
All inputs are finite; a program needn't handle non-finite values.
Results may differ from the reference program's by a relative error of at most 0.0001.
Values sent between devices are 32-bit elements; how exact they have to be, the bound alone decides.
No kernel may reach another device: no remote copies, remote signals or barrier semaphores. Data moves between devices by JAX's collectives and lax.ppermute only.
A program may use at most 64 MiB of HBM per device.

```python
import jax
import jax.numpy as jnp
from jax import lax

W = 1024
O = 1000
BAT_DEV = 16
P_DEV = 2048
CENTRES = 32768
BATCH = 256
POINTS = 32768


def scaled_rows(key, rows, cols):
    first, second = jax.random.split(key)
    base = jax.random.normal(first, (rows, cols), jnp.float32)
    scales = jnp.exp(jax.random.uniform(second, (rows, 1), jnp.float32, jnp.log(0.25), jnp.log(1.0)))
    return jnp.clip(base * scales, -6.0, 6.0)


def draw_features(key, part):
    return scaled_rows(jax.random.fold_in(key, 11), POINTS, W)


def draw_centres(key, part):
    return scaled_rows(jax.random.fold_in(key, 23), CENTRES, W)


def plant(entries, stream_key, smallest, largest):
    longest = entries.shape.index(max(entries.shape))
    spots = []
    for shift in (0, 1):
        where = [jax.random.randint(jax.random.fold_in(stream_key, axis), (), 0, length) for axis, length in enumerate(entries.shape)]
        where[longest] = (where[longest] + shift) % entries.shape[longest]
        spots.append(tuple(where))
    return entries.at[spots[0]].set(smallest).at[spots[1]].set(largest)


def levels(own_key, dims, pieces, least, largest):
    loudness = 1.0
    for dim, parts in pieces:
        draws = jax.random.uniform(jax.random.fold_in(jax.random.fold_in(own_key, 6), dim), (parts,), jnp.float32, least / len(pieces), largest / len(pieces))
        loudness = loudness * jnp.repeat(jnp.exp(draws), dims[dim] // parts).reshape((-1,) + (1,) * (len(dims) - 1 - dim))
    return loudness


def scatter_about(key, dims, scale, limit, pieces=(), held_as=jnp.bfloat16):
    gain = levels(key, dims, pieces, -0.22, 0.18) if pieces else 1.0
    drawn = jax.random.normal(key, dims, jnp.float32) * scale * gain
    return jnp.minimum(jnp.maximum(drawn, -limit), limit).astype(held_as)


def setup_inputs(seed: int = 0) -> dict:
    splits = jax.random.split(jax.random.key(seed), 6)
    return {
        "features": draw_features(jax.random.fold_in(splits[5], 71), 0),
        "centres": draw_centres(jax.random.fold_in(splits[5], 71), 0),
        "coefs": scatter_about(splits[2], (CENTRES, O), (CENTRES // 4) ** -0.5, 0.0625, ((0, 16), (1, 2)), jnp.float32),
        "batch_index": plant(jax.random.randint(splits[3], (2, BATCH), 0, P_DEV), jax.random.fold_in(splits[3], 1), 0, P_DEV - 1).astype(jnp.int32),
        "targets": scatter_about(splits[4], (2, BATCH, O), 1.0, 6.0, ((1, 16), (2, 2)), jnp.float32),
    }


def kernel_rows(batch, centres):
    batch_sq = lax.optimization_barrier(jnp.sum(batch * batch, axis=1))
    centre_sq = lax.optimization_barrier(jnp.sum(centres * centres, axis=1))
    inner = lax.dot_general(batch, centres, (((1,), (1,)), ((), ())), precision=lax.Precision.HIGHEST, preferred_element_type=jnp.float32)
    squared = batch_sq[:, None] + centre_sq[None, :] - 2.0 * inner
    return jnp.exp(-jnp.sqrt(jnp.maximum(squared, 0.0)) / (0.5 * jnp.sqrt(jnp.float32(W))))

def reference(features, centres, coefs, batch_index, targets):
    owner = jnp.arange(BATCH, dtype=jnp.int32) // BAT_DEV * P_DEV
    new_coefs = coefs
    results = []
    for step in range(2):
        rows = features[owner + batch_index[step]]
        kern = kernel_rows(rows, centres)
        predict = jnp.dot(kern, coefs, precision=lax.Precision.HIGHEST, preferred_element_type=jnp.float32)
        resid = predict - targets[step]
        results.append(resid)
        grad = lax.dot_general(kern, resid, (((0,), (0,)), ((), ())), precision=lax.Precision.HIGHEST, preferred_element_type=jnp.float32) / BATCH
        scale = jnp.sqrt(jnp.sum(grad * grad) / (CENTRES * O) + 1e-06)
        new_coefs = new_coefs - 0.1 * grad / scale
    return (jnp.stack(results), new_coefs)
```

```python
import math

import jax
import jax.numpy as jnp
from jax import lax
from jax.sharding import PartitionSpec as P

SHARE = 4


def product(left, right, dims, precision):
    return lax.dot_general(
        left,
        right,
        (dims, ((), ())),
        precision=precision,
        preferred_element_type=jnp.float32,
    )


def partial_squares(batch, centres):
    batch_sq = jnp.sum(batch * batch, axis=1)
    centre_sq = jnp.sum(centres * centres, axis=1)
    inner = product(batch, centres, ((1,), (1,)), lax.Precision.HIGHEST)
    return batch_sq[:, None] + centre_sq[None, :] - 2.0 * inner


def laplace(squared, width):
    return jnp.exp(-jnp.sqrt(jnp.maximum(squared, 0.0)) / (0.5 * math.sqrt(width)))


def swap(x, bit):
    n = lax.axis_size("cen")
    return lax.ppermute(x, "cen", [(i, i ^ bit) for i in range(n)])


def others(x):
    n = lax.axis_size("out")
    return [lax.ppermute(x, "out", [(i, (i + s) % n) for i in range(n)]) for s in range(1, n)]


def sum_out(x):
    if lax.axis_size("out") > 2:
        return lax.psum(x, "out")
    for part in others(x):
        x = x + part
    return x


def bits():
    n = lax.axis_size("cen")
    return [1 << b for b in range(n.bit_length() - 1)]


def gather(x):
    rest = x.shape
    for bit in reversed(bits()):
        x = jnp.stack([x, swap(x, bit)])
    return x.reshape((-1,) + rest[1:])


def scatter_sum(x):
    n = lax.axis_size("cen")
    x = x.reshape((n, -1) + x.shape[1:])
    for bit in bits():
        half = x.shape[0] // 2
        halves = x.reshape((2, half) + x.shape[1:])
        x = halves[0] + swap(halves[1], bit)
    return x[0]


def total(x):
    for part in others(x):
        x = x + part
    for bit in bits():
        x = x + swap(x, bit)
    return x


def body(features, centres, coefs, batch_index, targets):
    local_rows = batch_index.shape[1]
    batch_total = local_rows * lax.axis_size("cen")
    width = features.shape[1] * lax.axis_size("out")
    entries = centres.shape[0] * lax.axis_size("cen") * coefs.shape[1] * lax.axis_size("out")
    pair = lax.axis_size("out") <= 2
    sent = centres.shape[0] // SHARE if pair else 0
    early, late = centres[:sent], centres[sent:]

    picked = [jnp.take(features, batch_index[step], axis=0) for step in range(2)]
    own = [gather(picked[step]) for step in range(2)]
    if pair:
        far_centres = others(early)
        far_rows = [gather(rows) for rows in others(jnp.concatenate(picked))]

    kerns = []
    for step in range(2):
        late_sq = sum_out(partial_squares(own[step], late))
        if not pair:
            kerns.append(laplace(late_sq, width))
            continue
        early_sq = partial_squares(own[step], early)
        for rows, far in zip(far_rows, far_centres):
            rows = rows.reshape((-1, 2, local_rows, rows.shape[1]))[:, step]
            early_sq = early_sq + partial_squares(rows.reshape((-1, rows.shape[-1])), far)
        kerns.append(jnp.concatenate([laplace(early_sq, width), laplace(late_sq, width)], axis=1))

    results = []
    new_coefs = coefs
    for step in range(2):
        predicted = product(kerns[step], coefs, ((1,), (0,)), lax.Precision.HIGH)
        resid = scatter_sum(predicted) - targets[step]
        results.append(resid)
        grad = product(kerns[step], gather(resid), ((0,), (0,)), lax.Precision.HIGH) / batch_total
        scale = jnp.sqrt(total(jnp.sum(grad * grad)) / entries + 1e-06)
        new_coefs = new_coefs - 0.1 * grad / scale
    return (jnp.stack(results), new_coefs)


def solution(mesh):
    placed = (
        P("cen", "out"),
        P("cen", "out"),
        P("cen", "out"),
        P(None, "cen"),
        P(None, "cen", "out"),
    )
    return jax.shard_map(
        body,
        mesh=mesh,
        in_specs=placed,
        out_specs=(P(None, "cen", "out"), P("cen", "out")),
        check_vma=False,
    )
```

```python
import math

import jax
import jax.numpy as jnp
from jax import lax
from jax.sharding import PartitionSpec as P

SHARE = (3, 8)


def product(left, right, dims, precision):
    return lax.dot_general(
        left,
        right,
        (dims, ((), ())),
        precision=precision,
        preferred_element_type=jnp.float32,
    )


def partial_squares(batch, centres):
    batch_sq = jnp.sum(batch * batch, axis=1)
    centre_sq = jnp.sum(centres * centres, axis=1)
    inner = product(batch, centres, ((1,), (1,)), lax.Precision.HIGHEST)
    return batch_sq[:, None] + centre_sq[None, :] - 2.0 * inner


def laplace(squared, width):
    return jnp.exp(-jnp.sqrt(jnp.maximum(squared, 0.0)) / (0.5 * math.sqrt(width)))


def swap(x, bit):
    n = lax.axis_size("cen")
    return lax.ppermute(x, "cen", [(i, i ^ bit) for i in range(n)])


def others(x):
    n = lax.axis_size("out")
    return [lax.ppermute(x, "out", [(i, (i + s) % n) for i in range(n)]) for s in range(1, n)]


def sum_out(x):
    if lax.axis_size("out") > 2:
        return lax.psum(x, "out")
    for part in others(x):
        x = x + part
    return x


def after(x, first):
    return lax.optimization_barrier((x, first))[0]


def bits():
    n = lax.axis_size("cen")
    return [1 << b for b in range(n.bit_length() - 1)]


def mine(bit):
    return (lax.axis_index("cen") & bit) != 0


def place():
    index = lax.axis_index("cen")
    spot = 0
    for bit in bits():
        spot = 2 * spot + jnp.where((index & bit) != 0, 1, 0)
    return spot


def pair_up(x, bit):
    far = swap(x, bit)
    return jnp.where(mine(bit), jnp.stack([far, x]), jnp.stack([x, far]))


def gather(x):
    rest = x.shape
    for bit in reversed(bits()):
        x = pair_up(x, bit)
    return x.reshape((-1,) + rest)


def sum_cen(x):
    halves = x.reshape((2, x.shape[0] // 2) + x.shape[1:])
    side = jnp.where(mine(1), 1, 0)
    part = halves[side] + swap(halves[1 - side], 1)
    early = None
    for bit in bits()[1:]:
        part = part + swap(part, bit)
        early = part if early is None else early
    return pair_up(part, 1).reshape(x.shape), early


def chunks(local_rows):
    half = local_rows // 2
    return [(0, 0, local_rows), (1, 0, half), (1, half, local_rows)]


def body(features, centres, coefs, batch_index, targets):
    local_rows = batch_index.shape[1]
    batch_total = local_rows * lax.axis_size("cen")
    outputs = coefs.shape[1]
    width = features.shape[1] * lax.axis_size("out")
    entries = centres.shape[0] * lax.axis_size("cen") * outputs * lax.axis_size("out")
    pair = lax.axis_size("out") <= 2
    sent = centres.shape[0] * SHARE[0] // SHARE[1] if pair else 0
    early, late = centres[:sent], centres[sent:]

    picked = [jnp.take(features, batch_index[step], axis=0) for step in range(2)]
    own = [gather(picked[0])]
    rest = [picked[1]]
    if pair:
        far_centres = others(early)
        rest += others(jnp.concatenate(picked))
    rest = gather(after(jnp.concatenate(rest), own[0]))
    own.append(rest[:, :local_rows])

    partial = []
    for step, first, last in chunks(local_rows):
        rows = own[step][:, first:last].reshape(-1, features.shape[1])
        if partial:
            rows = after(rows, partial[-1])
        partial.append(partial_squares(rows, late))
    squares = [sum_out(part) for part in partial]

    spot = place()
    done = {0: [], 1: []}
    gate = None
    for (step, first, last), square in zip(chunks(local_rows), squares):
        kern = laplace(square if gate is None else after(square, gate), width)
        if pair:
            rows = own[step][:, first:last].reshape(-1, features.shape[1])
            early_sq = partial_squares(rows, early)
            for index, far in enumerate(far_centres):
                start = (1 + 2 * index + step) * local_rows
                rows = rest[:, start + first : start + last].reshape(-1, features.shape[1])
                early_sq = early_sq + partial_squares(rows, far)
            kern = jnp.concatenate([laplace(early_sq, width), kern], axis=1)
        predicted = product(kern, coefs, ((1,), (0,)), lax.Precision.HIGH)
        owner = lax.broadcasted_iota(jnp.int32, (lax.axis_size("cen"), 1, 1), 0)
        share = jnp.where(owner == spot, targets[step, first:last][None], 0.0)
        sent_on = [predicted - share.reshape(predicted.shape)]
        for before, _, _ in done[step]:
            sent_on.append(product(kern, before, ((1,), (1,)), lax.Precision.HIGHEST))
        sent_on.append(product(kern, kern, ((1,), (1,)), lax.Precision.HIGHEST))
        summed, gate = sum_cen(jnp.concatenate(sent_on, axis=1))
        done[step].append((kern, summed[:, :outputs], summed[:, outputs:]))

    results = []
    new_coefs = coefs
    for step in range(2):
        square = 0.0
        grad = 0.0
        resids = []
        for place_in, (kern, resid, inner) in enumerate(done[step]):
            column = 0
            for before, (_, other, _) in enumerate(done[step][: place_in + 1]):
                alike = product(resid, other, ((1,), (1,)), lax.Precision.HIGHEST)
                once = jnp.sum(inner[:, column : column + other.shape[0]] * alike)
                square = square + (once if before == place_in else 2.0 * once)
                column += other.shape[0]
            grad = grad + product(kern, resid, ((0,), (0,)), lax.Precision.HIGH)
            rows = resid.reshape(lax.axis_size("cen"), -1, outputs)
            resids.append(lax.dynamic_index_in_dim(rows, spot, 0, keepdims=False))
        results.append(jnp.concatenate(resids))
        square = jnp.maximum(sum_out(square), 0.0) / (batch_total * batch_total)
        scale = jnp.sqrt(square / entries + 1e-06)
        new_coefs = new_coefs - grad * (0.1 / batch_total / scale)
    return (jnp.stack(results), new_coefs)


def solution(mesh):
    placed = (
        P("cen", "out"),
        P("cen", "out"),
        P("cen", "out"),
        P(None, "cen"),
        P(None, "cen", "out"),
    )
    return jax.shard_map(
        body,
        mesh=mesh,
        in_specs=placed,
        out_specs=(P(None, "cen", "out"), P("cen", "out")),
        check_vma=False,
    )
```

```python
import functools
import math

import jax
import jax.numpy as jnp
from jax import lax
from jax.experimental import pallas as pl
from jax.experimental.pallas import tpu as pltpu
from jax.sharding import PartitionSpec as P

BLOCK = 256
SHARE = (1, 2)
LIMIT = 48 << 20
ROWS = ((1,), (1,))
ANY = pl.BlockSpec(memory_space=pl.ANY)
SCALARS = pl.BlockSpec(memory_space=pltpu.SMEM)


def dot(left, right, dims):
    return lax.dot_general(
        left, right, (dims, ((), ())), precision=lax.Precision.HIGHEST, preferred_element_type=jnp.float32
    )


def halves(x):
    high = x.astype(jnp.bfloat16)
    return high, (x - high.astype(jnp.float32)).astype(jnp.bfloat16)


def dot3(left, right, dims):
    one = functools.partial(lax.dot_general, dimension_numbers=(dims, ((), ())), preferred_element_type=jnp.float32)
    return one(left[0], right[0]) + (one(left[0], right[1]) + one(left[1], right[0]))


def laplace(squared, width):
    return jnp.exp(-jnp.sqrt(jnp.maximum(squared, 0.0)) / (0.5 * math.sqrt(width)))


def whole(x):
    return pl.BlockSpec(x.shape, lambda *_: (0,) * len(x.shape))


def call(kernel, grid, in_specs, out_specs, out_shape, scratch, flops, size):
    return pl.pallas_call(
        kernel,
        grid=grid,
        in_specs=in_specs,
        out_specs=out_specs,
        out_shape=out_shape,
        scratch_shapes=scratch,
        compiler_params=pltpu.CompilerParams(vmem_limit_bytes=LIMIT),
        cost_estimate=pl.CostEstimate(flops=flops, bytes_accessed=size, transcendentals=0),
    )


def f32(*shape):
    return jax.ShapeDtypeStruct(shape, jnp.float32)


def take(features, centres, batch_index, first, last):
    steps, rows = batch_index.shape
    copied = last > first

    def kernel(index, table, source, *rest):
        out = rest[0]
        sems = rest[-1]
        copies = []
        if copied:
            copies.append(pltpu.make_async_copy(source.at[pl.ds(first, last - first)], rest[1], sems.at[steps * rows]))
        for step in range(steps):
            for row in range(rows):
                spot = step * rows + row
                copies.append(
                    pltpu.make_async_copy(
                        table.at[pl.ds(index[step, row], 1)], out.at[pl.ds(spot, 1)], sems.at[spot]
                    )
                )
        for copy in copies:
            copy.start()
        for copy in copies:
            copy.wait()

    width = features.shape[1]
    shapes = [f32(steps * rows, width)] + ([f32(last - first, width)] if copied else [])
    return call(
        kernel, (), [SCALARS, ANY, ANY], [ANY] * len(shapes), shapes,
        [pltpu.SemaphoreType.DMA((steps * rows + 1,))], 0, 4 * width * (rows * steps + last - first),
    )(batch_index, features, centres)


def chunk_rows(ref, ranges):
    width = ref.shape[-1]
    return jnp.concatenate([ref[:, a:b].reshape(-1, width) for a, b in ranges])


def square_sums(x):
    return jnp.sum(x * x, axis=1, keepdims=True)


def square_row(x):
    return dot(jnp.ones((8, x.shape[1]), jnp.float32), x * x, ROWS)[:1]


def partial_squares(own, ranges, centres, start, order=()):
    count = own.shape[0]
    sizes = [count * (b - a) for a, b in ranges]
    late = centres.shape[0] - start

    def kernel(own_ref, centre_ref, *rest):
        outs = rest[len(order):]
        rows = chunk_rows(own_ref, ranges)
        block = centre_ref[...]
        square = square_sums(rows) + square_row(block) - 2.0 * dot(rows, block, ROWS)
        top = 0
        for out, size in zip(outs, sizes):
            out[...] = square[top : top + size]
            top += size

    total = sum(sizes)
    return call(
        kernel, (late // BLOCK,),
        [whole(own), pl.BlockSpec((BLOCK, own.shape[2]), lambda i: (i + start // BLOCK, 0))] + [ANY] * len(order),
        [pl.BlockSpec((size, BLOCK), lambda i: (0, i)) for size in sizes],
        [f32(size, late) for size in sizes],
        [], 12 * total * late * own.shape[2], 4 * (late * own.shape[2] + total * late),
    )(own, centres, *order)


def early_kernel(own, far, ranges, centres, fetched, width):
    sizes = [own.shape[0] * (b - a) for a, b in ranges]
    starts = [0]
    for part in fetched:
        starts.append(starts[-1] + part.shape[0] // BLOCK)

    def kernel(own_ref, far_ref, centre_ref, *rest):
        step = pl.program_id(0)
        outs = rest[len(fetched):]
        rows, others = chunk_rows(own_ref, ranges), chunk_rows(far_ref, ranges)
        block = centre_ref[...]
        near = square_sums(rows) + square_row(block) - 2.0 * dot(rows, block, ROWS)
        away = rest[0][...]
        for index in range(1, len(fetched)):
            away = jnp.where(step >= starts[index], rest[index][...], away)
        square = near + (square_sums(others) + square_row(away) - 2.0 * dot(others, away, ROWS))
        kern = laplace(square, width)
        top = 0
        for out, size in zip(outs, sizes):
            out[...] = kern[top : top + size]
            top += size

    def placed(index):
        blocks = starts[index + 1] - starts[index]
        return lambda i: (jnp.clip(i - starts[index], 0, blocks - 1), 0)

    depth = own.shape[2]
    total = sum(sizes)
    early = starts[-1] * BLOCK
    return call(
        kernel, (starts[-1],),
        [whole(own), whole(far), pl.BlockSpec((BLOCK, depth), lambda i: (i, 0))]
        + [pl.BlockSpec((BLOCK, depth), placed(index)) for index in range(len(fetched))],
        [pl.BlockSpec((size, BLOCK), lambda i: (0, i)) for size in sizes],
        [f32(size, early) for size in sizes],
        [], 24 * total * early * depth, 8 * early * depth + 4 * total * early,
    )(own, far, centres, *fetched)


def padded(outputs):
    return -(-outputs // 128) * 128


def predict(where, early, squares, coefs, targets, before, width, order=()):
    rows = squares[0].shape[0]
    centres, outputs = coefs.shape
    early_blocks = 0 if early is None else early.shape[1] // BLOCK
    pad = padded(outputs)
    columns = pad + sum(x.shape[0] for x in before) + rows
    own = targets.shape[0]
    quarter = rows // 4
    steps = centres // BLOCK
    ins = ([] if early is None else [early]) + list(squares) + [coefs, targets] + list(before) + list(order)

    def kernel(where_ref, *rest):
        rest = list(rest)
        early_ref = rest.pop(0) if early_blocks else None
        square_refs = [rest.pop(0) for _ in squares]
        coefs_ref, target_ref = rest.pop(0), rest.pop(0)
        before_refs = [rest.pop(0) for _ in before]
        kern_ref, out_ref, total = rest[len(order):]
        step = pl.program_id(0)

        @pl.when(step == 0)
        def _():
            total[...] = jnp.zeros_like(total)

        def late():
            square = square_refs[0][...]
            for ref in square_refs[1:]:
                square = square + ref[...]
            kern_ref[...] = laplace(square, width)

        if early_blocks:
            @pl.when(step < early_blocks)
            def _():
                kern_ref[...] = early_ref[...]

            pl.when(step >= early_blocks)(late)
        else:
            late()
        kern = halves(kern_ref[...])
        total[:, :outputs] += dot3(kern, halves(coefs_ref[...]), ((1,), (0,)))
        top = pad
        for ref in before_refs:
            total[:, top : top + ref.shape[0]] += dot3(kern, halves(ref[...]), ROWS)
            top += ref.shape[0]
        total[:, top:] += dot3(kern, kern, ROWS)

        @pl.when(step == steps - 1)
        def _():
            mine = pl.ds(pl.multiple_of(where_ref[0] * own, own), own)
            total[mine, :outputs] -= target_ref[...]
            for block in range(4):
                source = pl.multiple_of((where_ref[1] ^ block) * quarter, quarter)
                out_ref[block] = total[pl.ds(source, quarter), :]

    late_map = lambda i: (0, jnp.maximum(i - early_blocks, 0))
    specs = [SCALARS]
    if early_blocks:
        specs.append(pl.BlockSpec((rows, BLOCK), lambda i: (0, jnp.minimum(i, early_blocks - 1))))
    specs += [pl.BlockSpec((rows, BLOCK), late_map) for _ in squares]
    specs += [pl.BlockSpec((BLOCK, outputs), lambda i: (i, 0)), whole(targets)]
    specs += [pl.BlockSpec((x.shape[0], BLOCK), lambda i: (0, i)) for x in before]
    specs += [ANY] * len(order)
    return call(
        kernel, (steps,), specs,
        [pl.BlockSpec((rows, BLOCK), lambda i: (0, i)), pl.BlockSpec((4, quarter, columns), lambda i: (0, 0, 0))],
        [f32(rows, centres), f32(4, quarter, columns)],
        [pltpu.VMEM((rows, columns), jnp.float32)],
        6 * rows * centres * columns, 4 * centres * (outputs + 3 * rows),
    )(where, *ins)


def settle(where, near, far, outputs, own, before, square):
    quarter = near.shape[1]
    rows = 4 * quarter
    pad = padded(outputs)
    inner_columns = near.shape[2] - pad
    ins = [near, far] + list(before) + ([] if square is None else [square])

    def kernel(where_ref, near_ref, far_ref, *rest):
        before_refs = rest[: len(before)]
        resid_ref, own_ref, square_ref, inner = rest[-4:]
        for block in range(4):
            ref = (near_ref, far_ref)[block // 2]
            spot = pl.ds(pl.multiple_of((where_ref[1] ^ block) * quarter, quarter), quarter)
            resid_ref[spot, :] = ref[block % 2, :, :outputs]
            inner[spot, :] = ref[block % 2, :, pad:]
        resid = resid_ref[...]
        total = 0.0
        top = 0
        for ref in before_refs:
            part = inner[:, top : top + ref.shape[0]] * dot(resid, ref[...], ROWS)
            total = total + 2.0 * jnp.sum(part)
            top += ref.shape[0]
        total = total + jnp.sum(inner[:, top:] * dot(resid, resid, ROWS))
        if square is not None:
            square_ref[...] = rest[len(before)][...] + total
        else:
            square_ref[...] = jnp.full(square_ref.shape, total)
        own_ref[...] = resid_ref[pl.ds(pl.multiple_of(where_ref[0] * own, own), own), :]

    shapes = [f32(rows, outputs), f32(own, outputs), f32(8, 128)]
    return call(
        kernel, (1,), [SCALARS] + [whole(x) for x in ins], [whole(x) for x in shapes], shapes,
        [pltpu.VMEM((rows, inner_columns), jnp.float32)],
        12 * rows * inner_columns * outputs, 4 * near.size * 3,
    )(where, *ins)


def update(coefs, kerns, resids, squares, batch_total, entries):
    centres, outputs = coefs.shape
    count = len(kerns)

    def kernel(coefs_ref, *rest):
        square = rest[2 * count][:1, :1]
        for ref in rest[2 * count + 1 : -1]:
            square = square + ref[:1, :1]
        square = jnp.maximum(square, 0.0) / (batch_total * batch_total)
        scale = jnp.sqrt(square / entries + 1e-06)
        grad = 0.0
        for kern_ref, resid_ref in zip(rest[:count], rest[count:]):
            grad = grad + dot3(halves(kern_ref[...]), halves(resid_ref[...]), ((0,), (0,)))
        rest[-1][...] = coefs_ref[...] - (0.1 / batch_total) * grad / scale

    block = pl.BlockSpec((BLOCK, outputs), lambda i: (i, 0))
    rows = sum(x.shape[0] for x in kerns)
    return call(
        kernel, (centres // BLOCK,),
        [block] + [pl.BlockSpec((x.shape[0], BLOCK), lambda i: (0, i)) for x in kerns]
        + [whole(x) for x in list(resids) + list(squares)],
        block, f32(centres, outputs), [], 6 * rows * centres * outputs, 4 * centres * (rows + 2 * outputs),
    )(coefs, *kerns, *resids, *squares)


def swap(x, bit):
    n = lax.axis_size("cen")
    return lax.ppermute(x, "cen", [(i, i ^ bit) for i in range(n)])


def across(x):
    return lax.ppermute(x, "out", [(0, 1), (1, 0)])


def bits():
    n = lax.axis_size("cen")
    return [1 << b for b in range(n.bit_length() - 1)]


def mine(bit):
    return (lax.axis_index("cen") & bit) != 0


def gather(x):
    rest = x.shape
    for bit in reversed(bits()):
        far = swap(x, bit)
        x = jnp.where(mine(bit), jnp.stack([far, x]), jnp.stack([x, far]))
    return x.reshape((-1,) + rest)


def sum_cen(x):
    x = x[:2] + swap(x[2:], 1)
    first = x[0] + swap(x[1], 2)
    x = first
    for bit in bits()[2:]:
        x = x + swap(x, bit)
    x = jnp.stack([x, swap(x, 2)])
    return x, swap(x, 1), first


def body(features, centres, coefs, batch_index, targets):
    local_rows = batch_index.shape[1]
    devices = lax.axis_size("cen")
    batch_total = local_rows * devices
    outputs = coefs.shape[1]
    width = features.shape[1] * lax.axis_size("out")
    entries = centres.shape[0] * devices * outputs * lax.axis_size("out")
    pair = lax.axis_size("out") == 2
    sent = centres.shape[0] * SHARE[0] // SHARE[1] if pair else 0
    half = local_rows // 2
    chunks = [(0, 0, local_rows), (1, 0, half), (1, half, local_rows)]
    ranges = [(step * local_rows + a, step * local_rows + b) for step, a, b in chunks]

    place = 0
    for bit in bits():
        place = 2 * place + jnp.where(mine(bit), 1, 0)
    where = jnp.stack([place, 2 * jnp.where(mine(1), 1, 0) + jnp.where(mine(2), 1, 0)]).astype(jnp.int32)

    if pair:
        fetched = [across(centres[:BLOCK])]
        picked, more = take(features, centres, batch_index, BLOCK, sent)
        far = across(picked)
        fetched.append(across(more))
        own = gather(picked)
        far = gather(far)
    else:
        own = gather(take(features, centres, batch_index, 0, 0)[0])

    first = partial_squares(own, ranges[:1], centres, sent)
    partial = list(first) + list(partial_squares(own, ranges[1:], centres, sent, first))
    if pair:
        squares = [[x, across(x)] for x in partial]
        early = early_kernel(own, far, ranges, centres, fetched, width)
    else:
        squares = [[lax.psum(x, "out")] for x in partial]
        early = [None] * len(chunks)

    kerns, resids, results, sums = [[], []], [[], []], [], [None, None]
    gates = []
    for (step, a, b), near, square in zip(chunks, early, squares):
        kern, blocks = predict(where, near, square, coefs, targets[step, a:b], kerns[step], width, gates)
        summed, far_summed, gate = sum_cen(blocks)
        gates = [gate]
        resid, rows, sums[step] = settle(where, summed, far_summed, outputs, b - a, resids[step], sums[step])
        kerns[step].append(kern)
        resids[step].append(resid)
        results.append(rows)

    new_coefs = coefs
    for step in range(2):
        parts = [sums[step], across(sums[step])] if pair else [lax.psum(sums[step], "out")]
        new_coefs = update(new_coefs, kerns[step], resids[step], parts, batch_total, entries)
    return (jnp.stack([results[0], jnp.concatenate(results[1:])]), new_coefs)


def solution(mesh):
    placed = (
        P("cen", "out"),
        P("cen", "out"),
        P("cen", "out"),
        P(None, "cen"),
        P(None, "cen", "out"),
    )
    return jax.shard_map(
        body,
        mesh=mesh,
        in_specs=placed,
        out_specs=(P(None, "cen", "out"), P("cen", "out")),
        check_vma=False,
    )
```

```python
import functools
import math

import jax
import jax.numpy as jnp
from jax import lax
from jax.experimental import pallas as pl
from jax.experimental.pallas import tpu as pltpu
from jax.sharding import PartitionSpec as P

BLOCK = 256
SHARE = (1, 2)
LIMIT = 48 << 20
ROWS = ((1,), (1,))
ANY = pl.BlockSpec(memory_space=pl.ANY)
HBM = pl.BlockSpec(memory_space=pltpu.HBM)
SCALARS = pl.BlockSpec(memory_space=pltpu.SMEM)


def dot(left, right, dims):
    return lax.dot_general(
        left, right, (dims, ((), ())), precision=lax.Precision.HIGHEST, preferred_element_type=jnp.float32
    )


def halves(x):
    high = x.astype(jnp.bfloat16)
    return high, (x - high.astype(jnp.float32)).astype(jnp.bfloat16)


def joined(parts, axis):
    return parts[0] if len(parts) == 1 else jnp.concatenate(parts, axis=axis)


def dot3(left, right, dims):
    left = joined([x for high, low in left for x in (high, high, low)], dims[0][0])
    right = joined([x for high, low in right for x in (high, low, high)], dims[1][0])
    return lax.dot_general(left, right, (dims, ((), ())), preferred_element_type=jnp.float32)


def laplace(squared, width):
    return jnp.exp(-jnp.sqrt(jnp.maximum(squared, 0.0)) / (0.5 * math.sqrt(width)))


def whole(x):
    return pl.BlockSpec(x.shape, lambda *_: (0,) * len(x.shape))


def call(kernel, grid, in_specs, out_specs, out_shape, scratch, flops, size):
    return pl.pallas_call(
        kernel,
        grid=grid,
        in_specs=in_specs,
        out_specs=out_specs,
        out_shape=out_shape,
        scratch_shapes=scratch,
        compiler_params=pltpu.CompilerParams(vmem_limit_bytes=LIMIT),
        cost_estimate=pl.CostEstimate(flops=flops, bytes_accessed=size, transcendentals=0),
    )


def f32(*shape):
    return jax.ShapeDtypeStruct(shape, jnp.float32)


def take(features, centres, batch_index, first, last, order=()):
    steps, rows = batch_index.shape
    copied = last > first

    def kernel(index, table, source, *rest):
        rest = rest[len(order):]
        out = rest[0]
        sems = rest[-1]
        copies = []
        if copied:
            copies.append(pltpu.make_async_copy(source.at[pl.ds(first, last - first)], rest[1], sems.at[steps * rows]))
        for step in range(steps):
            for row in range(rows):
                spot = step * rows + row
                copies.append(
                    pltpu.make_async_copy(
                        table.at[pl.ds(index[step, row], 1)], out.at[pl.ds(spot, 1)], sems.at[spot]
                    )
                )
        for copy in copies:
            copy.start()
        for copy in copies:
            copy.wait()

    width = features.shape[1]
    shapes = [f32(steps * rows, width)] + ([f32(last - first, width)] if copied else [])
    return call(
        kernel, (), [SCALARS, HBM, HBM] + [ANY] * len(order), [pl.BlockSpec(memory_space=pltpu.VMEM)] * len(shapes), shapes,
        [pltpu.SemaphoreType.DMA((steps * rows + 1,))], 0, 4 * width * (rows * steps + last - first),
    )(batch_index, features, centres, *order)


def chunk_rows(ref, ranges):
    width = ref.shape[-1]
    return jnp.concatenate([ref[:, a:b].reshape(-1, width) for a, b in ranges])


def square_sums(x):
    return jnp.sum(x * x, axis=1, keepdims=True)


def square_row(x):
    return dot(jnp.ones((8, x.shape[1]), jnp.float32), x * x, ROWS)[:1]


def partial_squares(own, ranges, centres, start, order=()):
    count = own.shape[0]
    sizes = [count * (b - a) for a, b in ranges]
    late = centres.shape[0] - start

    def kernel(own_ref, centre_ref, *rest):
        outs = rest[len(order):]
        rows = chunk_rows(own_ref, ranges)
        block = centre_ref[...]
        square = square_sums(rows) + square_row(block) - 2.0 * dot3([halves(rows)], [halves(block)], ROWS)
        top = 0
        for out, size in zip(outs, sizes):
            out[...] = square[top : top + size]
            top += size

    total = sum(sizes)
    return call(
        kernel, (late // BLOCK,),
        [whole(own), pl.BlockSpec((BLOCK, own.shape[2]), lambda i: (i + start // BLOCK, 0))] + [ANY] * len(order),
        [pl.BlockSpec((size, BLOCK), lambda i: (0, i)) for size in sizes],
        [f32(size, late) for size in sizes],
        [], 12 * total * late * own.shape[2], 4 * (late * own.shape[2] + total * late),
    )(own, centres, *order)


def padded(outputs):
    return (outputs // 128 + 1) * 128


def add_products(total, kern, coefs, outputs):
    kern = halves(kern)
    total[:, :outputs] += dot3([kern], [halves(coefs)], ROWS)
    if total.shape[1] > padded(outputs):
        total[:, padded(outputs):] += dot3([kern], [kern], ROWS)


def early_part(own, far, local_rows, centres, fetched, coefs, width, order=()):
    devices, both_rows, depth = own.shape
    steps = both_rows // local_rows
    rows = devices * local_rows
    outputs = coefs.shape[0]
    columns = [padded(outputs)] * (steps - 1) + [padded(outputs) + rows]
    starts = [0]
    for part in fetched:
        starts.append(starts[-1] + part.shape[0] // BLOCK)
    ranges = [(step * local_rows, (step + 1) * local_rows) for step in range(steps)]

    def kernel(own_ref, far_ref, centre_ref, coefs_ref, *rest):
        step = pl.program_id(0)
        outs = rest[len(fetched) + len(order): -5]
        near_high, near_low, far_high, far_low, row_square = rest[-5:]

        @pl.when(step == 0)
        def _():
            near, others = chunk_rows(own_ref, ranges), chunk_rows(far_ref, ranges)
            near_high[...], near_low[...] = halves(near)
            far_high[...], far_low[...] = halves(others)
            row_square[...] = jnp.broadcast_to(square_sums(near) + square_sums(others), row_square.shape)

        block = centre_ref[...]
        away = rest[0][...]
        for index in range(1, len(fetched)):
            away = jnp.where(step >= starts[index], rest[index][...], away)
        centre_square = square_row(block) + square_row(away)
        block, away = halves(block), halves(away)
        pairs = [(near_high[...], near_low[...]), (far_high[...], far_low[...])]
        inner = dot3(pairs, [block, away], ROWS)
        kern = laplace(row_square[:, :1] + centre_square - 2.0 * inner, width)
        both = halves(kern)
        predicted = dot3([both], [halves(coefs_ref[...])], ROWS)
        for index in range(steps):
            kern_ref, total = outs[index], outs[steps + index]
            span = slice(index * rows, (index + 1) * rows)
            part = (both[0][span], both[1][span])
            kern_ref[...] = kern[span]

            @pl.when(step == 0)
            def _():
                total[...] = jnp.zeros_like(total)

            total[:, :outputs] += predicted[span]
            if total.shape[1] > padded(outputs):
                total[:, padded(outputs):] += dot3([part], [part], ROWS)

    def placed(index):
        blocks = starts[index + 1] - starts[index]
        return lambda i: (jnp.clip(i - starts[index], 0, blocks - 1), 0)

    early = starts[-1] * BLOCK
    result = call(
        kernel, (starts[-1],),
        [whole(own), whole(far), pl.BlockSpec((BLOCK, depth), lambda i: (i, 0)), pl.BlockSpec((outputs, BLOCK), lambda i: (0, i))]
        + [pl.BlockSpec((BLOCK, depth), placed(index)) for index in range(len(fetched))] + [ANY] * len(order),
        [pl.BlockSpec((rows, BLOCK), lambda i: (0, i))] * steps + [pl.BlockSpec((rows, wide), lambda i: (0, 0)) for wide in columns],
        [f32(rows, early)] * steps + [f32(rows, wide) for wide in columns],
        [pltpu.VMEM((steps * rows, depth), jnp.bfloat16)] * 4 + [pltpu.VMEM((steps * rows, 128), jnp.float32)],
        12 * steps * rows * early * depth, 8 * early * depth + 4 * steps * rows * early,
    )(own, far, centres, coefs, *fetched, *order)
    return list(zip(result[:steps], result[steps:]))


def predict(where, early, squares, coefs, targets, width, with_inner, order=()):
    rows, late = squares[0].shape
    outputs, centres = coefs.shape
    columns = padded(outputs) + (rows if with_inner else 0)
    own = targets.shape[0]
    quarter = rows // 4
    steps = late // BLOCK
    skipped = centres // BLOCK - steps
    given = [] if early is None else [early[1]]
    ins = list(squares) + [coefs, targets] + given + list(order)

    def kernel(where_ref, *rest):
        square_refs, rest = rest[: len(squares)], rest[len(squares):]
        coefs_ref, target_ref = rest[:2]
        kern_ref, out_ref, total = rest[-3:]
        step = pl.program_id(0)

        @pl.when(step == 0)
        def _():
            total[...] = rest[2][...] if given else jnp.zeros_like(total)

        square = square_refs[0][...]
        for ref in square_refs[1:]:
            square = square + ref[...]
        kern = laplace(square, width)
        kern_ref[...] = kern
        add_products(total, kern, coefs_ref[...], outputs)

        @pl.when(step == steps - 1)
        def _():
            mine = pl.ds(pl.multiple_of(where_ref[0] * own, own), own)
            total[mine, :outputs] -= target_ref[...]
            for block in range(4):
                source = pl.multiple_of((where_ref[1] ^ block) * quarter, quarter)
                out_ref[block] = total[pl.ds(source, quarter), :]

    specs = [SCALARS] + [pl.BlockSpec((rows, BLOCK), lambda i: (0, i)) for _ in squares]
    specs += [pl.BlockSpec((outputs, BLOCK), lambda i: (0, i + skipped)), whole(targets)]
    specs += [whole(x) for x in given]
    specs += [ANY] * len(order)
    return call(
        kernel, (steps,), specs,
        [pl.BlockSpec((rows, BLOCK), lambda i: (0, i)), pl.BlockSpec((4, quarter, columns), lambda i: (0, 0, 0))],
        [f32(rows, late), f32(4, quarter, columns)],
        [pltpu.VMEM((rows, columns), jnp.float32)],
        6 * rows * late * columns, 4 * late * (outputs + 3 * rows),
    )(where, *ins)


def settle(where, near, far, outputs, own):
    quarter = near.shape[1]
    rows = 4 * quarter
    pad = padded(outputs)
    with_inner = near.shape[2] > pad

    def kernel(where_ref, near_ref, far_ref, turned_ref, own_ref, *rest):
        resid_ref = rest[-1]
        inner = rest[1] if with_inner else None
        marked = jnp.zeros((1, 1), jnp.float32)
        for block in range(4):
            ref = (near_ref, far_ref)[block // 2]
            spot = pl.ds(pl.multiple_of((where_ref[1] ^ block) * quarter, quarter), quarter)
            resid_ref[spot, :] = ref[block % 2, :, :pad]
            if with_inner:
                inner[spot, :] = ref[block % 2, :, pad:]
                marked = marked + ref[block % 2, :1, pad - 1 : pad]
        resid = resid_ref[...]
        if with_inner:
            resid = jnp.where(lax.broadcasted_iota(jnp.int32, resid.shape, 1) < outputs, resid, 0.0)
            rest[0][:8, :] = jnp.broadcast_to(marked, (8, 128))
            rest[0][8:, :] = jnp.full((8, 128), jnp.sum(inner[...] * dot(resid, resid, ROWS)))
        turned_ref[...] = resid.T[:outputs]
        own_ref[...] = resid_ref[pl.ds(pl.multiple_of(where_ref[0] * own, own), own), :][:, :outputs]

    shapes = [f32(outputs, rows), f32(own, outputs)] + ([f32(16, 128)] if with_inner else [])
    scratch = [pltpu.VMEM((rows, rows), jnp.float32)] if with_inner else []
    return call(
        kernel, (1,), [SCALARS, whole(near), whole(far)], [whole(x) for x in shapes], shapes,
        scratch + [pltpu.VMEM((rows, pad), jnp.float32)],
        12 * rows * rows * outputs, 4 * near.size * 3,
    )(where, near, far)


def pieces(kerns):
    wide = math.gcd(*[x.shape[1] for x in kerns], 2 * BLOCK)
    starts = [0]
    for kern in kerns:
        starts.append(starts[-1] + kern.shape[1] // wide)

    def placed(index):
        blocks = starts[index + 1] - starts[index]
        return lambda i: (0, jnp.clip(i - starts[index], 0, blocks - 1))

    return wide, starts, [pl.BlockSpec((x.shape[0], wide), placed(index)) for index, x in enumerate(kerns)]


def product_of(turned_ref, kern_refs, starts):
    kern = kern_refs[0][...]
    for index in range(1, len(kern_refs)):
        kern = jnp.where(pl.program_id(0) >= starts[index], kern_refs[index][...], kern)
    return dot3([halves(turned_ref[...])], [halves(kern)], ((1,), (0,)))


def gradient(kerns, turned, mark_shape, column, order=()):
    outputs, rows = turned.shape
    centres = sum(x.shape[1] for x in kerns)
    wide, starts, specs = pieces(kerns)

    def kernel(turned_ref, *rest):
        out_ref, mark_ref, total = rest[len(kerns) + len(order):]
        grad = product_of(turned_ref, rest[: len(kerns)], starts)
        out_ref[...] = grad
        square = jnp.sum(grad * grad, axis=0, keepdims=True)

        @pl.when(pl.program_id(0) == 0)
        def _():
            total[...] = jnp.zeros_like(total)

        total[...] += square

        @pl.when(pl.program_id(0) == centres // wide - 1)
        def _():
            marked = lax.broadcasted_iota(jnp.int32, mark_shape, 1) == column
            mark_ref[...] = jnp.where(marked, jnp.sum(total[...]), 0.0)

    return call(
        kernel, (centres // wide,), [whole(turned)] + specs + [ANY] * len(order),
        [pl.BlockSpec((outputs, wide), lambda i: (0, i)), pl.BlockSpec(mark_shape, lambda i: (0, 0))],
        [f32(outputs, centres), f32(*mark_shape)], [pltpu.VMEM((1, wide), jnp.float32)],
        6 * rows * centres * outputs, 4 * centres * (rows + outputs),
    )(turned, *kerns, *order)


def update(coefs, grad, kerns, turned, squares, batch_total, entries):
    outputs, centres = coefs.shape
    rows = turned.shape[1]
    wide, starts, specs = pieces(kerns)

    def kernel(coefs_ref, grad_ref, turned_ref, *rest):
        kern_refs, square_refs = rest[: len(kerns)], rest[len(kerns) : -1]

        def factor(row):
            square = square_refs[0][row : row + 1, :1]
            for more in square_refs[1:]:
                square = square + more[row : row + 1, :1]
            square = jnp.maximum(square, 0.0) / (batch_total * batch_total)
            return 0.1 / batch_total / jnp.sqrt(square / entries + 1e-06)

        result = coefs_ref[...] - grad_ref[...] * factor(0)
        rest[-1][...] = result - product_of(turned_ref, kern_refs, starts) * factor(8)

    block = pl.BlockSpec((outputs, wide), lambda i: (0, i))
    return call(
        kernel, (centres // wide,), [block, block, whole(turned)] + specs + [whole(x) for x in squares],
        block, f32(outputs, centres), [], 6 * rows * centres * outputs, 4 * centres * (rows + 3 * outputs),
    )(coefs, grad, turned, *kerns, *squares)


def swap(x, bit):
    n = lax.axis_size("cen")
    return lax.ppermute(x, "cen", [(i, i ^ bit) for i in range(n)])


def across(x):
    return lax.ppermute(x, "out", [(0, 1), (1, 0)])


def bits():
    n = lax.axis_size("cen")
    return [1 << b for b in range(n.bit_length() - 1)]


def mine(bit):
    return (lax.axis_index("cen") & bit) != 0


def grow(x, bit):
    far = swap(x, bit)
    return jnp.where(mine(bit), jnp.stack([far, x]), jnp.stack([x, far]))


def gathered(x):
    return x.reshape((-1,) + x.shape[-2:])


def after(x, token):
    return jnp.where(token == token, x, token)


def gather(own, ahead=None, far=None):
    for step, bit in enumerate(reversed(bits())):
        own = grow(own, bit)
        if far is not None:
            if step == 0:
                own = after(own, ahead[: own.size // own.shape[-1]].reshape(own.shape))
            else:
                token = own
                while token.ndim > far.ndim:
                    token = token[0]
                far = grow(after(far, token), bits()[-step])
    if far is None:
        return gathered(own)
    return gathered(own), gathered(grow(far, bits()[0]))


def sum_half(x):
    return x[:2] + swap(x[2:], 1)


def sum_rest(x, mark=None):
    x = x[0] + swap(x[1], 2)
    if mark is not None:
        x = x + mark
    for bit in bits()[2:]:
        x = x + swap(x, bit)
    x = jnp.stack([x, swap(x, 2)])
    return x, swap(x, 1)


def body(features, centres, coefs, batch_index, targets):
    local_rows = batch_index.shape[1]
    devices = lax.axis_size("cen")
    batch_total = local_rows * devices
    outputs = coefs.shape[1]
    width = features.shape[1] * lax.axis_size("out")
    entries = centres.shape[0] * devices * outputs * lax.axis_size("out")
    pair = lax.axis_size("out") == 2
    sent = centres.shape[0] * SHARE[0] // SHARE[1] if pair else 0
    ranges = [(step * local_rows, (step + 1) * local_rows) for step in range(2)]
    coefs = coefs.T

    place = 0
    for bit in bits():
        place = 2 * place + jnp.where(mine(bit), 1, 0)
    where = jnp.stack([place, 2 * jnp.where(mine(1), 1, 0) + jnp.where(mine(2), 1, 0)]).astype(jnp.int32)

    if pair:
        ahead = centres[:BLOCK]
        fetched = [across(ahead)]
        picked, more = take(features, centres, batch_index, BLOCK, sent, [ahead])
        far = across(picked)
        fetched.append(across(more))
        own, far = gather(picked, fetched[0], far)
    else:
        own = gather(take(features, centres, batch_index, 0, 0)[0])

    partial = partial_squares(own, ranges[:1], centres, sent)
    partial = list(partial) + list(partial_squares(own, ranges[1:], centres, sent, partial))
    if pair:
        squares = [[x, across(x)] for x in partial]
        early = early_part(own, far, local_rows, centres, fetched, coefs, width, partial)
    else:
        squares = [[lax.psum(x, "out")] for x in partial]
        early = [None, None]

    def kernels(step, kern):
        return [kern] if early[step] is None else [early[step][0], kern]

    kern, blocks = predict(where, early[0], squares[0], coefs, targets[0], width, False)
    turned, rows, *_ = settle(where, *sum_rest(sum_half(blocks)), outputs, local_rows)
    kern_next, blocks = predict(where, early[1], squares[1], coefs, targets[1], width, True, [turned])
    blocks = sum_half(blocks)
    grad, mark = gradient(kernels(0, kern), turned, blocks.shape[1:], padded(outputs) - 1, [blocks])
    turned, rows_next, square = settle(where, *sum_rest(blocks, mark), outputs, local_rows)
    parts = [square, across(square)] if pair else [lax.psum(square, "out")]
    new_coefs = update(coefs, grad, kernels(1, kern_next), turned, parts, batch_total, entries)
    return (jnp.stack([rows, rows_next]), new_coefs.T)


def solution(mesh):
    placed = (
        P("cen", "out"),
        P("cen", "out"),
        P("cen", "out"),
        P(None, "cen"),
        P(None, "cen", "out"),
    )
    return jax.shard_map(
        body,
        mesh=mesh,
        in_specs=placed,
        out_specs=(P(None, "cen", "out"), P("cen", "out")),
        check_vma=False,
    )
```

```python
import functools
import math

import jax
import jax.numpy as jnp
from jax import lax
from jax.experimental import pallas as pl
from jax.experimental.pallas import tpu as pltpu
from jax.sharding import PartitionSpec as P

BLOCK = 256
SHARE = (1, 2)
LIMIT = 28 << 20
MOST = 60 << 20
STRIPS = 16
ROWS = ((1,), (1,))
ANY = pl.BlockSpec(memory_space=pl.ANY)
SCALARS = pl.BlockSpec(memory_space=pltpu.SMEM)


def dot(left, right, dims):
    return lax.dot_general(
        left, right, (dims, ((), ())), precision=lax.Precision.HIGHEST, preferred_element_type=jnp.float32
    )


def halves(x):
    high = x.astype(jnp.bfloat16)
    return high, (x - high.astype(jnp.float32)).astype(jnp.bfloat16)


def joined(parts, axis):
    return parts[0] if len(parts) == 1 else jnp.concatenate(parts, axis=axis)


def dot3(left, right, dims):
    left = joined([x for high, low in left for x in (high, high, low)], dims[0][0])
    right = joined([x for high, low in right for x in (high, low, high)], dims[1][0])
    return lax.dot_general(left, right, (dims, ((), ())), preferred_element_type=jnp.float32)


def laplace(squared, width):
    return jnp.exp(-jnp.sqrt(jnp.maximum(squared, 0.0)) / (0.5 * math.sqrt(width)))


def whole(x):
    return pl.BlockSpec(x.shape, lambda *_: (0,) * len(x.shape))


def call(kernel, grid, in_specs, out_specs, out_shape, scratch, flops, size, limit=LIMIT):
    return pl.pallas_call(
        kernel,
        grid=grid,
        in_specs=in_specs,
        out_specs=out_specs,
        out_shape=out_shape,
        scratch_shapes=scratch,
        compiler_params=pltpu.CompilerParams(vmem_limit_bytes=limit),
        cost_estimate=pl.CostEstimate(flops=flops, bytes_accessed=size, transcendentals=0),
    )


def f32(*shape):
    return jax.ShapeDtypeStruct(shape, jnp.float32)


def take(features, centres, batch_index, first, last, order=()):
    steps, rows = batch_index.shape
    copied = last > first

    def kernel(index, table, source, *rest):
        rest = rest[len(order):]
        out = rest[0]
        sems = rest[-1]
        copies = []
        if copied:
            copies.append(pltpu.make_async_copy(source.at[pl.ds(first, last - first)], rest[1], sems.at[steps * rows]))
        for step in range(steps):
            for row in range(rows):
                spot = step * rows + row
                copies.append(
                    pltpu.make_async_copy(
                        table.at[pl.ds(index[step, row], 1)], out.at[pl.ds(spot, 1)], sems.at[spot]
                    )
                )
        for copy in copies:
            copy.start()
        for copy in copies:
            copy.wait()

    width = features.shape[1]
    shapes = [f32(steps * rows, width)] + ([f32(last - first, width)] if copied else [])
    return call(
        kernel, (), [SCALARS, ANY, ANY] + [ANY] * len(order), [pl.BlockSpec(memory_space=pltpu.VMEM)] * len(shapes), shapes,
        [pltpu.SemaphoreType.DMA((steps * rows + 1,))], 0, 4 * width * (rows * steps + last - first), MOST,
    )(batch_index, features, centres, *order)


def chunk_rows(ref, ranges):
    width = ref.shape[-1]
    return jnp.concatenate([ref[:, a:b].reshape(-1, width) for a, b in ranges])


def square_sums(x):
    return jnp.sum(x * x, axis=1, keepdims=True)


def square_row(x):
    return dot(jnp.ones((8, x.shape[1]), jnp.float32), x * x, ROWS)[:1]


def partial_squares(own, span, centres, start, end, order=()):
    rows = own.shape[0] * (span[1] - span[0])

    def kernel(own_ref, centre_ref, *rest):
        part, block = chunk_rows(own_ref, [span]), centre_ref[...]
        square = square_sums(part) + square_row(block) - 2.0 * dot3([halves(part)], [halves(block)], ROWS)
        rest[-1][...] = square

    late = end - start
    return call(
        kernel, (late // BLOCK,),
        [whole(own), pl.BlockSpec((BLOCK, own.shape[2]), lambda i: (i + start // BLOCK, 0))] + [ANY] * len(order),
        pl.BlockSpec((rows, BLOCK), lambda i: (0, i)), f32(rows, late),
        [], 6 * rows * late * own.shape[2], 4 * (late * own.shape[2] + rows * late),
    )(own, centres, *order)


def padded(outputs):
    return (outputs // 128 + 1) * 128


def packs(rows, outputs):
    half = rows // STRIPS // 2
    return half % 8 == 0 and rows % 256 == 0 and half <= padded(outputs) - 1 - outputs


def inner_columns(rows, outputs):
    return rows // 2 if packs(rows, outputs) else rows


def packed(strip, index, lane):
    high, rows = strip.shape
    half = high // 2
    start = index * high

    def turned(first, to):
        return pltpu.roll(strip, (to - first) % rows, axis=1)

    if index < STRIPS // 2:
        rest = turned(start + rows // 2, lane)[:, :128]
    else:
        left = turned(start + rows // 2, lane)[half:, :128]
        right = turned(start + rows // 2 + half, lane)[half:, :128]
        rest = jnp.concatenate([right, left])
    column = lax.broadcasted_iota(jnp.int32, rest.shape, 1)
    used = (column >= lane) & (column < lane + half)
    return turned(start, 0)[:, : rows // 2], rest, used


def add_products(total, kern, coefs, outputs):
    kern = halves(kern)
    total[:, :outputs] += dot3([kern], [halves(coefs)], ROWS)
    if total.shape[1] > padded(outputs):
        total[:, padded(outputs):] += dot3([kern], [kern], ROWS)


def early_part(own, far, local_rows, centres, fetched, coefs, width, order=()):
    devices, both_rows, depth = own.shape
    steps = both_rows // local_rows
    rows = devices * local_rows
    outputs = coefs.shape[0]
    columns = [padded(outputs)] * (steps - 1) + [padded(outputs) + rows]
    starts = [0]
    for part in fetched:
        starts.append(starts[-1] + part.shape[0] // BLOCK)
    ranges = [(step * local_rows, (step + 1) * local_rows) for step in range(steps)]

    def kernel(own_ref, far_ref, centre_ref, coefs_ref, *rest):
        step = pl.program_id(0)
        outs = rest[len(fetched) + len(order): -5]
        near_high, near_low, far_high, far_low, row_square = rest[-5:]

        @pl.when(step == 0)
        def _():
            near, others = chunk_rows(own_ref, ranges), chunk_rows(far_ref, ranges)
            near_high[...], near_low[...] = halves(near)
            far_high[...], far_low[...] = halves(others)
            row_square[...] = jnp.broadcast_to(square_sums(near) + square_sums(others), row_square.shape)

        block = centre_ref[...]
        away = rest[0][...]
        for index in range(1, len(fetched)):
            away = jnp.where(step >= starts[index], rest[index][...], away)
        centre_square = square_row(block) + square_row(away)
        block, away = halves(block), halves(away)
        pairs = [(near_high[...], near_low[...]), (far_high[...], far_low[...])]
        inner = dot3(pairs, [block, away], ROWS)
        kern = laplace(row_square[:, :1] + centre_square - 2.0 * inner, width)
        both = halves(kern)
        predicted = dot3([both], [halves(coefs_ref[...])], ROWS)
        for index in range(steps):
            kern_ref, total = outs[index], outs[steps + index]
            span = slice(index * rows, (index + 1) * rows)
            part = (both[0][span], both[1][span])
            kern_ref[...] = kern[span]

            @pl.when(step == 0)
            def _():
                total[...] = jnp.zeros_like(total)

            total[:, :outputs] += predicted[span]
            if total.shape[1] > padded(outputs):
                total[:, padded(outputs):] += dot3([part], [part], ROWS)

    def placed(index):
        blocks = starts[index + 1] - starts[index]
        return lambda i: (jnp.clip(i - starts[index], 0, blocks - 1), 0)

    early = starts[-1] * BLOCK
    result = call(
        kernel, (starts[-1],),
        [whole(own), whole(far), pl.BlockSpec((BLOCK, depth), lambda i: (i, 0)), pl.BlockSpec((outputs, BLOCK), lambda i: (0, i))]
        + [pl.BlockSpec((BLOCK, depth), placed(index)) for index in range(len(fetched))] + [ANY] * len(order),
        [pl.BlockSpec((rows, BLOCK), lambda i: (0, i))] * steps + [pl.BlockSpec((rows, wide), lambda i: (0, 0)) for wide in columns],
        [f32(rows, early)] * steps + [f32(rows, wide) for wide in columns],
        [pltpu.VMEM((steps * rows, depth), jnp.bfloat16)] * 4 + [pltpu.VMEM((steps * rows, 128), jnp.float32)],
        12 * steps * rows * early * depth, 8 * early * depth + 4 * steps * rows * early,
    )(own, far, centres, coefs, *fetched, *order)
    return list(zip(result[:steps], result[steps:]))


def predict(where, given, squares, start, coefs, targets, width, with_inner, order=()):
    rows, late = squares[0].shape
    outputs, centres = coefs.shape
    columns = padded(outputs) + (rows if with_inner else 0)
    own = targets.shape[0]
    quarter = rows // 4
    steps = late // BLOCK
    pad = padded(outputs)
    sent = pad + inner_columns(rows, outputs) if with_inner else columns
    skipped = start // BLOCK
    last = start + late == centres
    given = [] if given is None else [given]
    ins = list(squares) + [coefs, targets] + given + list(order)

    def kernel(where_ref, *rest):
        square_refs, rest = rest[: len(squares)], rest[len(squares):]
        coefs_ref, target_ref = rest[0], rest[1]
        kern_ref, out_ref, total = rest[-3:]
        step = pl.program_id(0)

        @pl.when(step == 0)
        def _():
            total[...] = rest[2][...] if given else jnp.zeros_like(total)

        square = square_refs[0][...]
        for ref in square_refs[1:]:
            square = square + ref[...]
        kern = laplace(square, width)
        kern_ref[...] = kern
        add_products(total, kern, coefs_ref[...], outputs)

        @pl.when(step == steps - 1)
        def _():
            if last:
                mine = pl.ds(pl.multiple_of(where_ref[0] * own, own), own)
                total[mine, :outputs] -= target_ref[...]
                if sent < columns:
                    for index in range(STRIPS):
                        span = pl.ds(index * (rows // STRIPS), rows // STRIPS)
                        most, rest, used = packed(total[span, pad:], index, outputs % 128)
                        total[span, pad:sent] = most
                        total[span, pad - 128 : pad] = jnp.where(used, rest, total[span, pad - 128 : pad])
                for block in range(4):
                    source = pl.multiple_of((where_ref[1] ^ block) * quarter, quarter)
                    out_ref[block] = total[pl.ds(source, quarter), :sent]
            else:
                out_ref[...] = total[...]

    shape = f32(4, quarter, sent) if last else f32(rows, columns)
    specs = [SCALARS] + [pl.BlockSpec((rows, BLOCK), lambda i: (0, i)) for _ in squares]
    specs += [pl.BlockSpec((outputs, BLOCK), lambda i: (0, i + skipped)), whole(targets)]
    specs += [whole(x) for x in given] + [ANY] * len(order)
    return call(
        kernel, (steps,), specs,
        [pl.BlockSpec((rows, BLOCK), lambda i: (0, i)), whole(shape)],
        [f32(rows, late), shape],
        [pltpu.VMEM((rows, columns), jnp.float32)],
        6 * rows * late * columns, 4 * late * (outputs + 3 * rows),
    )(where, *ins)


def settle(where, near, far, outputs, own):
    quarter = near.shape[1]
    rows = 4 * quarter
    pad = padded(outputs)
    with_inner = near.shape[2] > pad

    def kernel(where_ref, near_ref, far_ref, turned_ref, own_ref, *rest):
        resid_ref = rest[-1]
        inner = rest[1] if with_inner else None
        marked = jnp.zeros((1, 1), jnp.float32)
        for block in range(4):
            ref = (near_ref, far_ref)[block // 2]
            spot = pl.ds(pl.multiple_of((where_ref[1] ^ block) * quarter, quarter), quarter)
            resid_ref[spot, :] = ref[block % 2, :, :pad]
            if with_inner:
                inner[spot, :] = ref[block % 2, :, pad:]
                marked = marked + ref[block % 2, :1, pad - 1 : pad]
        resid = resid_ref[...]
        if with_inner:
            resid = jnp.where(lax.broadcasted_iota(jnp.int32, resid.shape, 1) < outputs, resid, 0.0)
            rest[0][:8, :] = jnp.broadcast_to(marked, (8, 128))
            alike = dot(resid, resid, ROWS)
            if inner.shape[1] == rows:
                square = jnp.sum(inner[...] * alike)
            else:
                high = rows // STRIPS
                sums = jnp.zeros((high, rows // 2), jnp.float32)
                rests = jnp.zeros((high, 128), jnp.float32)
                for index in range(STRIPS):
                    span = slice(index * high, (index + 1) * high)
                    most, rest_of, used = packed(alike[span], index, outputs % 128)
                    sums = sums + most * inner[span, :]
                    rests = rests + jnp.where(used, rest_of * resid_ref[span, pad - 128 :], 0.0)
                diagonal = lax.broadcasted_iota(jnp.int32, sums.shape, 1) < high
                square = jnp.sum(jnp.where(diagonal, sums, 2.0 * sums)) + 2.0 * jnp.sum(rests)
            rest[0][8:, :] = jnp.full((8, 128), square)
        turned_ref[...] = resid.T[:outputs]
        own_ref[...] = resid_ref[pl.ds(pl.multiple_of(where_ref[0] * own, own), own), :][:, :outputs]

    shapes = [f32(outputs, rows), f32(own, outputs)] + ([f32(16, 128)] if with_inner else [])
    scratch = [pltpu.VMEM((rows, near.shape[2] - pad), jnp.float32)] if with_inner else []
    return call(
        kernel, (1,), [SCALARS, whole(near), whole(far)], [whole(x) for x in shapes], shapes,
        scratch + [pltpu.VMEM((rows, pad), jnp.float32)],
        12 * rows * rows * outputs, 4 * near.size * 3,
    )(where, near, far)


def pieces(kerns):
    wide = math.gcd(*[x.shape[1] for x in kerns], 2 * BLOCK)
    starts = [0]
    for kern in kerns:
        starts.append(starts[-1] + kern.shape[1] // wide)

    def placed(index):
        blocks = starts[index + 1] - starts[index]
        return lambda i: (0, jnp.clip(i - starts[index], 0, blocks - 1))

    return wide, starts, [pl.BlockSpec((x.shape[0], wide), placed(index)) for index, x in enumerate(kerns)]


def product_of(turned_ref, kern_refs, starts):
    kern = kern_refs[0][...]
    for index in range(1, len(kern_refs)):
        kern = jnp.where(pl.program_id(0) >= starts[index], kern_refs[index][...], kern)
    return dot3([halves(turned_ref[...])], [halves(kern)], ((1,), (0,)))


def gradient(kerns, turned, mark_shape, column, order=()):
    outputs, rows = turned.shape
    centres = sum(x.shape[1] for x in kerns)
    wide, starts, specs = pieces(kerns)

    def kernel(turned_ref, *rest):
        out_ref, mark_ref, total = rest[len(kerns) + len(order):]
        grad = product_of(turned_ref, rest[: len(kerns)], starts)
        out_ref[...] = grad
        square = jnp.sum(grad * grad, axis=0, keepdims=True)

        @pl.when(pl.program_id(0) == 0)
        def _():
            total[...] = jnp.zeros_like(total)

        total[...] += square

        @pl.when(pl.program_id(0) == centres // wide - 1)
        def _():
            marked = lax.broadcasted_iota(jnp.int32, mark_shape, 1) == column
            mark_ref[...] = jnp.where(marked, jnp.sum(total[...]), 0.0)

    return call(
        kernel, (centres // wide,), [whole(turned)] + specs + [ANY] * len(order),
        [pl.BlockSpec((outputs, wide), lambda i: (0, i)), pl.BlockSpec(mark_shape, lambda i: (0, 0))],
        [f32(outputs, centres), f32(*mark_shape)], [pltpu.VMEM((1, wide), jnp.float32)],
        6 * rows * centres * outputs, 4 * centres * (rows + outputs),
    )(turned, *kerns, *order)


def update(coefs, grad, kerns, turned, squares, batch_total, entries):
    outputs, centres = coefs.shape
    rows = turned.shape[1]
    wide, starts, specs = pieces(kerns)

    def kernel(coefs_ref, grad_ref, turned_ref, *rest):
        kern_refs, square_refs = rest[: len(kerns)], rest[len(kerns) : -1]

        def factor(row):
            square = square_refs[0][row : row + 1, :1]
            for more in square_refs[1:]:
                square = square + more[row : row + 1, :1]
            square = jnp.maximum(square, 0.0) / (batch_total * batch_total)
            return 0.1 / batch_total / jnp.sqrt(square / entries + 1e-06)

        result = coefs_ref[...] - grad_ref[...] * factor(0)
        rest[-1][...] = result - product_of(turned_ref, kern_refs, starts) * factor(8)

    block = pl.BlockSpec((outputs, wide), lambda i: (0, i))
    return call(
        kernel, (centres // wide,), [block, block, whole(turned)] + specs + [whole(x) for x in squares],
        block, f32(outputs, centres), [], 6 * rows * centres * outputs, 4 * centres * (rows + 3 * outputs),
    )(coefs, grad, turned, *kerns, *squares)


def swap(x, bit):
    n = lax.axis_size("cen")
    return lax.ppermute(x, "cen", [(i, i ^ bit) for i in range(n)])


def across(x):
    return lax.ppermute(x, "out", [(0, 1), (1, 0)])


def bits():
    n = lax.axis_size("cen")
    return [1 << b for b in range(n.bit_length() - 1)]


def mine(bit):
    return (lax.axis_index("cen") & bit) != 0


def grow(x, bit):
    far = swap(x, bit)
    return jnp.where(mine(bit), jnp.stack([far, x]), jnp.stack([x, far]))


def gathered(x):
    return x.reshape((-1,) + x.shape[-2:])


def after(x, token):
    return jnp.where(token == token, x, token)


def gather(own, ahead=None, far=None):
    for step, bit in enumerate(reversed(bits())):
        own = grow(own, bit)
        if far is not None:
            if step == 0:
                own = after(own, ahead[: own.size // own.shape[-1]].reshape(own.shape))
            else:
                token = own
                while token.ndim > far.ndim:
                    token = token[0]
                far = grow(after(far, token), bits()[-step])
    if far is None:
        return gathered(own)
    return gathered(own), gathered(grow(far, bits()[0]))


def sum_half(x):
    return x[:2] + swap(x[2:], 1)


def sum_rest(x, mark=None):
    x = x[0] + swap(x[1], 2)
    if mark is not None:
        x = x + mark
    for bit in bits()[2:]:
        x = x + swap(x, bit)
    x = jnp.stack([x, swap(x, 2)])
    return x, swap(x, 1)


def body(features, centres, coefs, batch_index, targets):
    local_rows = batch_index.shape[1]
    devices = lax.axis_size("cen")
    batch_total = local_rows * devices
    outputs = coefs.shape[1]
    width = features.shape[1] * lax.axis_size("out")
    entries = centres.shape[0] * devices * outputs * lax.axis_size("out")
    pair = lax.axis_size("out") == 2
    sent = centres.shape[0] * SHARE[0] // SHARE[1] if pair else 0
    ranges = [(step * local_rows, (step + 1) * local_rows) for step in range(2)]
    coefs = coefs.T

    place = 0
    for bit in bits():
        place = 2 * place + jnp.where(mine(bit), 1, 0)
    where = jnp.stack([place, 2 * jnp.where(mine(1), 1, 0) + jnp.where(mine(2), 1, 0)]).astype(jnp.int32)

    if pair:
        ahead = centres[:BLOCK]
        fetched = [across(ahead)]
        picked, more = take(features, centres, batch_index, BLOCK, sent, [ahead])
        far = across(picked)
        fetched.append(across(more))
        own, far = gather(picked, fetched[0], far)
    else:
        own = gather(take(features, centres, batch_index, 0, 0)[0])

    most, end = centres.shape[0] - BLOCK, centres.shape[0]
    partial = [[partial_squares(own, ranges[0], centres, sent, most)]]
    partial[0].append(partial_squares(own, ranges[0], centres, most, end, partial[0]))
    partial.append([partial_squares(own, ranges[1], centres, sent, end, partial[0][1:])])
    if pair:
        squares = [[[x, across(x)] for x in parts] for parts in partial]
        early = early_part(own, far, local_rows, centres, fetched, coefs, width, partial[1])
    else:
        squares = [[[lax.psum(x, "out")] for x in parts] for parts in partial]
        early = [None, None]

    def predicted(step, with_inner, order):
        kerns, out = ([], None) if early[step] is None else ([early[step][0]], early[step][1])
        start = sent
        for square in squares[step]:
            kern, out = predict(where, out, square, start, coefs, targets[step], width, with_inner, order)
            kerns.append(kern)
            start += kern.shape[1]
        return kerns, out

    kerns, blocks = predicted(0, False, [])
    turned, rows, *_ = settle(where, *sum_rest(sum_half(blocks)), outputs, local_rows)
    kerns_next, blocks = predicted(1, True, [turned])
    blocks = sum_half(blocks)
    grad, mark = gradient(kerns, turned, blocks.shape[1:], padded(outputs) - 1, [blocks])
    turned, rows_next, square = settle(where, *sum_rest(blocks, mark), outputs, local_rows)
    parts = [square, across(square)] if pair else [lax.psum(square, "out")]
    new_coefs = update(coefs, grad, kerns_next, turned, parts, batch_total, entries)
    return (jnp.stack([rows, rows_next]), new_coefs.T)


def solution(mesh):
    placed = (
        P("cen", "out"),
        P("cen", "out"),
        P("cen", "out"),
        P(None, "cen"),
        P(None, "cen", "out"),
    )
    return jax.shard_map(
        body,
        mesh=mesh,
        in_specs=placed,
        out_specs=(P(None, "cen", "out"), P("cen", "out")),
        check_vma=False,
    )
```

```python
import functools
import math

import jax
import jax.numpy as jnp
from jax import lax
from jax.experimental import pallas as pl
from jax.experimental.pallas import tpu as pltpu
from jax.sharding import PartitionSpec as P

BLOCK = 256
SHARE = (1, 2)
LIMIT = 28 << 20
MOST = 60 << 20
STRIPS = 16
ROWS = ((1,), (1,))
ANY = pl.BlockSpec(memory_space=pl.ANY)
SCALARS = pl.BlockSpec(memory_space=pltpu.SMEM)


def dot(left, right, dims):
    return lax.dot_general(
        left, right, (dims, ((), ())), precision=lax.Precision.HIGHEST, preferred_element_type=jnp.float32
    )


def halves(x):
    high = x.astype(jnp.bfloat16)
    return high, (x - high.astype(jnp.float32)).astype(jnp.bfloat16)


def joined(parts, axis):
    return parts[0] if len(parts) == 1 else jnp.concatenate(parts, axis=axis)


def dot3(left, right, dims):
    left = joined([x for high, low in left for x in (high, high, low)], dims[0][0])
    right = joined([x for high, low in right for x in (high, low, high)], dims[1][0])
    return lax.dot_general(left, right, (dims, ((), ())), preferred_element_type=jnp.float32)


def laplace(squared, width):
    return jnp.exp(-jnp.sqrt(jnp.maximum(squared, 0.0)) / (0.5 * math.sqrt(width)))


def whole(x):
    return pl.BlockSpec(x.shape, lambda *_: (0,) * len(x.shape))


def call(kernel, grid, in_specs, out_specs, out_shape, scratch, flops, size, limit=LIMIT):
    return pl.pallas_call(
        kernel,
        grid=grid,
        in_specs=in_specs,
        out_specs=out_specs,
        out_shape=out_shape,
        scratch_shapes=scratch,
        compiler_params=pltpu.CompilerParams(vmem_limit_bytes=limit),
        cost_estimate=pl.CostEstimate(flops=flops, bytes_accessed=size, transcendentals=0),
    )


def f32(*shape):
    return jax.ShapeDtypeStruct(shape, jnp.float32)


def take(features, centres, batch_index, first, last, order=()):
    steps, rows = batch_index.shape
    copied = last > first

    def kernel(index, table, source, *rest):
        rest = rest[len(order):]
        out = rest[0]
        sems = rest[-1]
        copies = []
        if copied:
            copies.append(pltpu.make_async_copy(source.at[pl.ds(first, last - first)], rest[1], sems.at[steps * rows]))
        for step in range(steps):
            for row in range(rows):
                spot = step * rows + row
                copies.append(
                    pltpu.make_async_copy(
                        table.at[pl.ds(index[step, row], 1)], out.at[pl.ds(spot, 1)], sems.at[spot]
                    )
                )
        for copy in copies:
            copy.start()
        for copy in copies:
            copy.wait()

    width = features.shape[1]
    shapes = [f32(steps * rows, width)] + ([f32(last - first, width)] if copied else [])
    return call(
        kernel, (), [SCALARS, ANY, ANY] + [ANY] * len(order), [pl.BlockSpec(memory_space=pltpu.VMEM)] * len(shapes), shapes,
        [pltpu.SemaphoreType.DMA((steps * rows + 1,))], 0, 4 * width * (rows * steps + last - first), MOST,
    )(batch_index, features, centres, *order)


def chunk_rows(ref, ranges):
    width = ref.shape[-1]
    return jnp.concatenate([ref[:, a:b].reshape(-1, width) for a, b in ranges])


def square_sums(x):
    return jnp.sum(x * x, axis=1, keepdims=True)


def square_row(x):
    return dot(jnp.ones((8, x.shape[1]), jnp.float32), x * x, ROWS)[:1]


def partial_squares(own, span, centres, start, end, order=()):
    rows = own.shape[0] * (span[1] - span[0])

    def kernel(own_ref, centre_ref, *rest):
        part, block = chunk_rows(own_ref, [span]), centre_ref[...]
        square = square_sums(part) + square_row(block) - 2.0 * dot3([halves(part)], [halves(block)], ROWS)
        rest[-1][...] = square

    late = end - start
    return call(
        kernel, (late // BLOCK,),
        [whole(own), pl.BlockSpec((BLOCK, own.shape[2]), lambda i: (i + start // BLOCK, 0))] + [ANY] * len(order),
        pl.BlockSpec((rows, BLOCK), lambda i: (0, i)), f32(rows, late),
        [], 6 * rows * late * own.shape[2], 4 * (late * own.shape[2] + rows * late),
    )(own, centres, *order)


def padded(outputs):
    return (outputs // 128 + 1) * 128


def packs(rows, outputs):
    half = rows // STRIPS // 2
    return half % 8 == 0 and rows % 256 == 0 and half <= padded(outputs) - 1 - outputs


def inner_columns(rows, outputs):
    return rows // 2 if packs(rows, outputs) else rows


def packed(strip, index, lane):
    high, rows = strip.shape
    half = high // 2
    start = index * high

    def turned(first, to):
        return pltpu.roll(strip, (to - first) % rows, axis=1)

    if index < STRIPS // 2:
        rest = turned(start + rows // 2, lane)[:, :128]
    else:
        left = turned(start + rows // 2, lane)[half:, :128]
        right = turned(start + rows // 2 + half, lane)[half:, :128]
        rest = jnp.concatenate([right, left])
    column = lax.broadcasted_iota(jnp.int32, rest.shape, 1)
    used = (column >= lane) & (column < lane + half)
    return turned(start, 0)[:, : rows // 2], rest, used


def add_products(total, kern, coefs, outputs):
    kern = halves(kern)
    total[:, :outputs] += dot3([kern], [halves(coefs)], ROWS)
    if total.shape[1] > padded(outputs):
        total[:, padded(outputs):] += dot3([kern], [kern], ROWS)


def early_part(own, far, local_rows, centres, fetched, coefs, width, order=()):
    devices, both_rows, depth = own.shape
    steps = both_rows // local_rows
    rows = devices * local_rows
    outputs = coefs.shape[0]
    columns = [padded(outputs)] * (steps - 1) + [padded(outputs) + rows]
    starts = [0]
    for part in fetched:
        starts.append(starts[-1] + part.shape[0] // BLOCK)
    ranges = [(step * local_rows, (step + 1) * local_rows) for step in range(steps)]

    def kernel(own_ref, far_ref, centre_ref, coefs_ref, *rest):
        step = pl.program_id(0)
        outs = rest[len(fetched) + len(order): -5]
        near_high, near_low, far_high, far_low, row_square = rest[-5:]

        @pl.when(step == 0)
        def _():
            near, others = chunk_rows(own_ref, ranges), chunk_rows(far_ref, ranges)
            near_high[...], near_low[...] = halves(near)
            far_high[...], far_low[...] = halves(others)
            row_square[...] = jnp.broadcast_to(square_sums(near) + square_sums(others), row_square.shape)

        block = centre_ref[...]
        away = rest[0][...]
        for index in range(1, len(fetched)):
            away = jnp.where(step >= starts[index], rest[index][...], away)
        centre_square = square_row(block) + square_row(away)
        block, away = halves(block), halves(away)
        pairs = [(near_high[...], near_low[...]), (far_high[...], far_low[...])]
        inner = dot3(pairs, [block, away], ROWS)
        kern = laplace(row_square[:, :1] + centre_square - 2.0 * inner, width)
        both = halves(kern)
        predicted = dot3([both], [halves(coefs_ref[...])], ROWS)
        for index in range(steps):
            kern_ref, total = outs[index], outs[steps + index]
            span = slice(index * rows, (index + 1) * rows)
            part = (both[0][span], both[1][span])
            kern_ref[...] = kern[span]

            @pl.when(step == 0)
            def _():
                total[...] = jnp.zeros_like(total)

            total[:, :outputs] += predicted[span]
            if total.shape[1] > padded(outputs):
                total[:, padded(outputs):] += dot3([part], [part], ROWS)

    def placed(index):
        blocks = starts[index + 1] - starts[index]
        return lambda i: (jnp.clip(i - starts[index], 0, blocks - 1), 0)

    early = starts[-1] * BLOCK
    result = call(
        kernel, (starts[-1],),
        [whole(own), whole(far), pl.BlockSpec((BLOCK, depth), lambda i: (i, 0)), pl.BlockSpec((outputs, BLOCK), lambda i: (0, i))]
        + [pl.BlockSpec((BLOCK, depth), placed(index)) for index in range(len(fetched))] + [ANY] * len(order),
        [pl.BlockSpec((rows, BLOCK), lambda i: (0, i))] * steps + [pl.BlockSpec((rows, wide), lambda i: (0, 0)) for wide in columns],
        [f32(rows, early)] * steps + [f32(rows, wide) for wide in columns],
        [pltpu.VMEM((steps * rows, depth), jnp.bfloat16)] * 4 + [pltpu.VMEM((steps * rows, 128), jnp.float32)],
        12 * steps * rows * early * depth, 8 * early * depth + 4 * steps * rows * early,
    )(own, far, centres, coefs, *fetched, *order)
    return list(zip(result[:steps], result[steps:]))


def predict(where, given, squares, start, coefs, targets, width, with_inner, order=()):
    rows, late = squares[0].shape
    outputs, centres = coefs.shape
    columns = padded(outputs) + (rows if with_inner else 0)
    own = targets.shape[0]
    quarter = rows // 4
    wide = math.gcd(late, start, 2 * BLOCK)
    steps = late // wide
    pad = padded(outputs)
    sent = pad + inner_columns(rows, outputs) if with_inner else columns
    skipped = start // wide
    last = start + late == centres
    given = [] if given is None else [given]
    ins = list(squares) + [coefs, targets] + given + list(order)

    def kernel(where_ref, *rest):
        square_refs, rest = rest[: len(squares)], rest[len(squares):]
        coefs_ref, target_ref = rest[0], rest[1]
        kern_ref, out_ref, total = rest[-3:]
        step = pl.program_id(0)

        @pl.when(step == 0)
        def _():
            total[...] = rest[2][...] if given else jnp.zeros_like(total)

        square = square_refs[0][...]
        for ref in square_refs[1:]:
            square = square + ref[...]
        kern = laplace(square, width)
        kern_ref[...] = kern
        add_products(total, kern, coefs_ref[...], outputs)

        @pl.when(step == steps - 1)
        def _():
            if last:
                mine = pl.ds(pl.multiple_of(where_ref[0] * own, own), own)
                total[mine, :outputs] -= target_ref[...]
                if sent < columns:
                    for index in range(STRIPS):
                        span = pl.ds(index * (rows // STRIPS), rows // STRIPS)
                        most, rest, used = packed(total[span, pad:], index, outputs % 128)
                        total[span, pad:sent] = most
                        total[span, pad - 128 : pad] = jnp.where(used, rest, total[span, pad - 128 : pad])
                for block in range(4):
                    source = pl.multiple_of((where_ref[1] ^ block) * quarter, quarter)
                    out_ref[block] = total[pl.ds(source, quarter), :sent]
            else:
                out_ref[...] = total[...]

    shape = f32(4, quarter, sent) if last else f32(rows, columns)
    specs = [SCALARS] + [pl.BlockSpec((rows, wide), lambda i: (0, i)) for _ in squares]
    specs += [pl.BlockSpec((outputs, wide), lambda i: (0, i + skipped)), whole(targets)]
    specs += [whole(x) for x in given] + [ANY] * len(order)
    return call(
        kernel, (steps,), specs,
        [pl.BlockSpec((rows, wide), lambda i: (0, i)), whole(shape)],
        [f32(rows, late), shape],
        [pltpu.VMEM((rows, columns), jnp.float32)],
        6 * rows * late * columns, 4 * late * (outputs + 3 * rows),
    )(where, *ins)


def settle(where, near, far, outputs, own):
    quarter = near.shape[1]
    rows = 4 * quarter
    pad = padded(outputs)
    with_inner = near.shape[2] > pad

    def kernel(where_ref, near_ref, far_ref, turned_ref, own_ref, *rest):
        resid_ref = rest[-1]
        inner = rest[1] if with_inner else None
        marked = jnp.zeros((1, 1), jnp.float32)
        for block in range(4):
            ref = (near_ref, far_ref)[block // 2]
            spot = pl.ds(pl.multiple_of((where_ref[1] ^ block) * quarter, quarter), quarter)
            resid_ref[spot, :] = ref[block % 2, :, :pad]
            if with_inner:
                inner[spot, :] = ref[block % 2, :, pad:]
                marked = marked + ref[block % 2, :1, pad - 1 : pad]
        resid = resid_ref[...]
        if with_inner:
            resid = jnp.where(lax.broadcasted_iota(jnp.int32, resid.shape, 1) < outputs, resid, 0.0)
            rest[0][:8, :] = jnp.broadcast_to(marked, (8, 128))
            alike = dot(resid, resid, ROWS)
            if inner.shape[1] == rows:
                square = jnp.sum(inner[...] * alike)
            else:
                high = rows // STRIPS
                sums = jnp.zeros((high, rows // 2), jnp.float32)
                rests = jnp.zeros((high, 128), jnp.float32)
                for index in range(STRIPS):
                    span = slice(index * high, (index + 1) * high)
                    most, rest_of, used = packed(alike[span], index, outputs % 128)
                    sums = sums + most * inner[span, :]
                    rests = rests + jnp.where(used, rest_of * resid_ref[span, pad - 128 :], 0.0)
                diagonal = lax.broadcasted_iota(jnp.int32, sums.shape, 1) < high
                square = jnp.sum(jnp.where(diagonal, sums, 2.0 * sums)) + 2.0 * jnp.sum(rests)
            rest[0][8:, :] = jnp.full((8, 128), square)
        turned_ref[...] = resid.T[:outputs]
        own_ref[...] = resid_ref[pl.ds(pl.multiple_of(where_ref[0] * own, own), own), :][:, :outputs]

    shapes = [f32(outputs, rows), f32(own, outputs)] + ([f32(16, 128)] if with_inner else [])
    scratch = [pltpu.VMEM((rows, near.shape[2] - pad), jnp.float32)] if with_inner else []
    return call(
        kernel, (1,), [SCALARS, whole(near), whole(far)], [whole(x) for x in shapes], shapes,
        scratch + [pltpu.VMEM((rows, pad), jnp.float32)],
        12 * rows * rows * outputs, 4 * near.size * 3,
    )(where, near, far)


def pieces(kerns):
    wide = math.gcd(*[x.shape[1] for x in kerns], 2 * BLOCK)
    starts = [0]
    for kern in kerns:
        starts.append(starts[-1] + kern.shape[1] // wide)

    def placed(index):
        blocks = starts[index + 1] - starts[index]
        return lambda i: (0, jnp.clip(i - starts[index], 0, blocks - 1))

    return wide, starts, [pl.BlockSpec((x.shape[0], wide), placed(index)) for index, x in enumerate(kerns)]


def product_of(turned_ref, kern_refs, starts):
    kern = kern_refs[0][...]
    for index in range(1, len(kern_refs)):
        kern = jnp.where(pl.program_id(0) >= starts[index], kern_refs[index][...], kern)
    return dot3([halves(turned_ref[...])], [halves(kern)], ((1,), (0,)))


def gradient(kerns, turned, mark_shape, column, order=()):
    outputs, rows = turned.shape
    centres = sum(x.shape[1] for x in kerns)
    wide, starts, specs = pieces(kerns)

    def kernel(turned_ref, *rest):
        out_ref, mark_ref, total = rest[len(kerns) + len(order):]
        grad = product_of(turned_ref, rest[: len(kerns)], starts)
        out_ref[...] = grad
        square = jnp.sum(grad * grad, axis=0, keepdims=True)

        @pl.when(pl.program_id(0) == 0)
        def _():
            total[...] = jnp.zeros_like(total)

        total[...] += square

        @pl.when(pl.program_id(0) == centres // wide - 1)
        def _():
            marked = lax.broadcasted_iota(jnp.int32, mark_shape, 1) == column
            mark_ref[...] = jnp.where(marked, jnp.sum(total[...]), 0.0)

    return call(
        kernel, (centres // wide,), [whole(turned)] + specs + [ANY] * len(order),
        [pl.BlockSpec((outputs, wide), lambda i: (0, i)), pl.BlockSpec(mark_shape, lambda i: (0, 0))],
        [f32(outputs, centres), f32(*mark_shape)], [pltpu.VMEM((1, wide), jnp.float32)],
        6 * rows * centres * outputs, 4 * centres * (rows + outputs),
    )(turned, *kerns, *order)


def update(coefs, grad, kerns, turned, squares, batch_total, entries):
    outputs, centres = coefs.shape
    rows = turned.shape[1]
    wide, starts, specs = pieces(kerns)

    def kernel(coefs_ref, grad_ref, turned_ref, *rest):
        kern_refs, square_refs = rest[: len(kerns)], rest[len(kerns) : -1]

        def factor(row):
            square = square_refs[0][row : row + 1, :1]
            for more in square_refs[1:]:
                square = square + more[row : row + 1, :1]
            square = jnp.maximum(square, 0.0) / (batch_total * batch_total)
            return 0.1 / batch_total / jnp.sqrt(square / entries + 1e-06)

        result = coefs_ref[...] - grad_ref[...] * factor(0)
        rest[-1][...] = result - product_of(turned_ref, kern_refs, starts) * factor(8)

    block = pl.BlockSpec((outputs, wide), lambda i: (0, i))
    return call(
        kernel, (centres // wide,), [block, block, whole(turned)] + specs + [whole(x) for x in squares],
        block, f32(outputs, centres), [], 6 * rows * centres * outputs, 4 * centres * (rows + 3 * outputs),
    )(coefs, grad, turned, *kerns, *squares)


def swap(x, bit):
    n = lax.axis_size("cen")
    return lax.ppermute(x, "cen", [(i, i ^ bit) for i in range(n)])


def across(x):
    return lax.ppermute(x, "out", [(0, 1), (1, 0)])


def bits():
    n = lax.axis_size("cen")
    return [1 << b for b in range(n.bit_length() - 1)]


def mine(bit):
    return (lax.axis_index("cen") & bit) != 0


def grow(x, bit):
    far = swap(x, bit)
    return jnp.where(mine(bit), jnp.stack([far, x]), jnp.stack([x, far]))


def gathered(x):
    return x.reshape((-1,) + x.shape[-2:])


def after(x, token):
    return jnp.where(token == token, x, token)


def gather(own, ahead=None, far=None):
    for step, bit in enumerate(reversed(bits())):
        own = grow(own, bit)
        if far is not None:
            if step == 0:
                own = after(own, ahead[: own.size // own.shape[-1]].reshape(own.shape))
            else:
                token = own
                while token.ndim > far.ndim:
                    token = token[0]
                far = grow(after(far, token), bits()[-step])
    if far is None:
        return gathered(own)
    return gathered(own), gathered(grow(far, bits()[0]))


def sum_half(x):
    return x[:2] + swap(x[2:], 1)


def sum_rest(x, mark=None):
    x = x[0] + swap(x[1], 2)
    if mark is not None:
        x = x + mark
    for bit in bits()[2:]:
        x = x + swap(x, bit)
    x = jnp.stack([x, swap(x, 2)])
    return x, swap(x, 1)


def body(features, centres, coefs, batch_index, targets):
    local_rows = batch_index.shape[1]
    devices = lax.axis_size("cen")
    batch_total = local_rows * devices
    outputs = coefs.shape[1]
    width = features.shape[1] * lax.axis_size("out")
    entries = centres.shape[0] * devices * outputs * lax.axis_size("out")
    pair = lax.axis_size("out") == 2
    sent = centres.shape[0] * SHARE[0] // SHARE[1] if pair else 0
    ranges = [(step * local_rows, (step + 1) * local_rows) for step in range(2)]
    coefs = coefs.T

    place = 0
    for bit in bits():
        place = 2 * place + jnp.where(mine(bit), 1, 0)
    where = jnp.stack([place, 2 * jnp.where(mine(1), 1, 0) + jnp.where(mine(2), 1, 0)]).astype(jnp.int32)

    if pair:
        ahead = centres[:BLOCK]
        fetched = [across(ahead)]
        picked, more = take(features, centres, batch_index, BLOCK, sent, [ahead])
        far = across(picked)
        fetched.append(across(more))
        own, far = gather(picked, fetched[0], far)
    else:
        own = gather(take(features, centres, batch_index, 0, 0)[0])

    most, end = centres.shape[0] - 2 * BLOCK, centres.shape[0]
    partial = [[partial_squares(own, ranges[0], centres, sent, most)]]
    partial[0].append(partial_squares(own, ranges[0], centres, most, end, partial[0]))
    partial.append([partial_squares(own, ranges[1], centres, sent, end, partial[0][1:])])
    if pair:
        squares = [[[x, across(x)] for x in parts] for parts in partial]
        early = early_part(own, far, local_rows, centres, fetched, coefs, width, partial[1])
    else:
        squares = [[[lax.psum(x, "out")] for x in parts] for parts in partial]
        early = [None, None]

    def predicted(step, with_inner, order):
        kerns, out = ([], None) if early[step] is None else ([early[step][0]], early[step][1])
        start = sent
        for square in squares[step]:
            kern, out = predict(where, out, square, start, coefs, targets[step], width, with_inner, order)
            kerns.append(kern)
            start += kern.shape[1]
        return kerns, out

    kerns, blocks = predicted(0, False, [])
    near, away = sum_rest(sum_half(blocks))
    turned, rows, *_ = settle(where, near, away, outputs, local_rows)
    kerns_next, blocks = predicted(1, True, [near])
    blocks = sum_half(blocks)
    grad, mark = gradient(kerns, turned, blocks.shape[1:], padded(outputs) - 1, [blocks])
    turned, rows_next, square = settle(where, *sum_rest(blocks, mark), outputs, local_rows)
    parts = [square, across(square)] if pair else [lax.psum(square, "out")]
    new_coefs = update(coefs, grad, kerns_next, turned, parts, batch_total, entries)
    return (jnp.stack([rows, rows_next]), new_coefs.T)


def solution(mesh):
    placed = (
        P("cen", "out"),
        P("cen", "out"),
        P("cen", "out"),
        P(None, "cen"),
        P(None, "cen", "out"),
    )
    return jax.shard_map(
        body,
        mesh=mesh,
        in_specs=placed,
        out_specs=(P(None, "cen", "out"), P("cen", "out")),
        check_vma=False,
    )
```
